32 devices in a mesh: groups: 2 (over y), space: 16 (over z, x, core).
Axes of the slice: x: 2, y: 2, z: 4, core: 2. Of those that a mesh axis runs over, the one named last changes fastest.
Arguments:
- block_features: bfloat16 [64, 64, 4096], P(('groups', 'space')), parts along dimension 0
- cotangent: bfloat16 [64, 64, 4096], P(('groups', 'space')), parts along dimension 0
- coords: int32 [64, 3], P('groups'), parts along dimension 0, may hold values from -1 to 255, as said below
- conv1_weight: bfloat16 [64, 1728], replicated, may hold values from -0.15625 to 0.15625
- conv1_bias: float32 [64], replicated, may hold values from -1 to 1
- conv2_weight: bfloat16 [64, 1728], replicated, may hold values from -0.15625 to 0.15625
Outputs:
- grad_features: bfloat16 [64, 64, 4096], P(('groups', 'space')), parts along dimension 0
- grad_conv1_weight: float32 [128, 1728], P('groups'), parts along dimension 0
- grad_conv2_weight: float32 [128, 1728], P('groups'), parts along dimension 0
- grad_conv1_bias: float32 [128], P('groups'), parts along dimension 0
The draws below stay inside these ranges and needn't reach their ends.
There are 2 independent parts, one for each index of `groups`. The reference program is written for one: setup_inputs(seed, part) draws one part's arguments, and reference() takes and returns one part's arrays. A program takes and returns all parts, laid end to end along the dimension named above; an argument that names none is the same for every part. Nothing has to cross between parts.
Inputs may be any that keep to these rules, and one draw needn't show every extreme that they name: `coords`: the rows of slab i are slots i * 2 to i * 2 + 1; an active slot of slab i has first coordinate i; empty slots hold -1 in all three coordinates; the active slots of a slab come before its empty ones; no two active slots share coordinates; slabs i and i + 8 hold at most 2 active blocks together.
All inputs are finite; a program needn't handle non-finite values.
Results may differ from the reference program's by a relative error of at most 0.0055.
Values may be sent and summed in bfloat16 or wider, within the bound.
A program may use at most 128 MiB of HBM per device.

```python
import math
import jax
import jax.numpy as jnp
import numpy as np
from jax import lax

CH = 64
BLOCK = 16
SLOT_DEV = 2
GRID = 256
SLABS = 16
SLOTS = 32


def channel_field(key):
    scale_key, value_key = jax.random.split(key, 2)
    scales = jnp.exp(jax.random.uniform(scale_key, (CH,), jnp.float32, math.log(0.3), math.log(3.0)))
    values = jax.random.normal(value_key, (SLOTS, CH, BLOCK ** 3), jnp.float32)
    return (values * scales[None, :, None]).astype(jnp.bfloat16)


def draw_block_features(key, part):
    return channel_field(jax.random.fold_in(key, 11))


def draw_cotangent(key, part):
    return channel_field(jax.random.fold_in(key, 23))


def draw_coords(key, part):
    half_count = SLABS // 2
    key_total, key_lower, key_walk = jax.random.split(jax.random.fold_in(key, 37), 3)
    pair_total = jnp.where(jax.random.randint(key_total, (half_count,), 0, 5) == 0, 1, 2).astype(jnp.int32)
    pair_total = pair_total.at[0].set(2).at[1].set(2).at[half_count - 1].set(2)
    lower_count = jax.random.randint(key_lower, (half_count,), 0, 3).astype(jnp.int32) % (pair_total + 1)
    lower_count = lower_count.at[0].set(1).at[1].set(2).at[half_count - 1].set(2)
    counts = jnp.concatenate([lower_count, pair_total - lower_count])
    moves = jax.random.randint(key_walk, (4, SLABS), -1, 2).astype(jnp.int32)
    starts = jnp.array([GRID // 4, GRID // 2, 3 * GRID // 4, GRID - 1], jnp.int32)
    steps_taken = jnp.cumsum(moves, axis=1) - moves
    walks = starts[:, None] + steps_taken - steps_taken[:, half_count:half_count + 1]
    slab_ids = jnp.arange(SLABS, dtype=jnp.int32)
    first_slot = jnp.stack([slab_ids, jnp.clip(walks[0], 0, GRID // 2 - 1), jnp.clip(walks[1], 0, GRID - 1)], axis=1)
    second_slot = jnp.stack([slab_ids, jnp.clip(walks[2], GRID // 2, GRID - 1), jnp.clip(walks[3], 0, GRID - 1)], axis=1)
    first_slot = jnp.where((counts >= 1)[:, None], first_slot, -1)
    second_slot = jnp.where((counts >= 2)[:, None], second_slot, -1)
    return jnp.stack([first_slot, second_slot], axis=1).reshape(SLABS * SLOT_DEV, 3).astype(jnp.int32)


def normal_values(own_key, extent, scale, most, kind=jnp.bfloat16):
    return jnp.clip(scale * jax.random.normal(own_key, extent, jnp.float32), -most, most).astype(kind)


def setup_inputs(seed: int = 0, part: int = 0) -> dict:
    seeds = jax.random.split(jax.random.key(seed), 7)
    own_keys = jax.random.split(jax.random.fold_in(seeds[6], part), 7)
    block_features = draw_block_features(jax.random.fold_in(jax.random.fold_in(seeds[6], part), 71), part)
    cotangent = draw_cotangent(jax.random.fold_in(jax.random.fold_in(seeds[6], part), 71), part)
    coords = draw_coords(jax.random.fold_in(jax.random.fold_in(seeds[6], part), 71), part)
    conv1_weight = normal_values(seeds[3], (CH, 27 * CH), (27 * CH) ** -0.5, 0.15625)
    conv1_bias = jnp.clip(jax.random.uniform(seeds[4], (CH,), jnp.float32, -1.0, 1.0), -1.0, 1.0)
    conv2_weight = normal_values(seeds[5], (CH, 27 * CH), (27 * CH) ** -0.5, 0.15625)
    return dict(block_features=block_features, cotangent=cotangent, coords=coords, conv1_weight=conv1_weight, conv1_bias=conv1_bias, conv2_weight=conv2_weight)


neighbour_steps = np.stack(np.meshgrid(np.arange(-1, 2), np.arange(-1, 2), np.arange(-1, 2), indexing='ij'), -1).reshape(27, 3).astype(np.int32)
clip_norm = 256.0

def trimmed(region, offset_step, axis_number, block_edge):
    if offset_step < 0:
        return lax.slice_in_dim(region, block_edge - 2, block_edge, axis=axis_number)
    if offset_step > 0:
        return lax.slice_in_dim(region, 0, 2, axis=axis_number)
    return region

def conv_valid(inputs, kernel, upcast):
    if upcast:
        inputs = inputs.astype(jnp.float32)
        kernel = kernel.astype(jnp.float32)
    return lax.conv_general_dilated(inputs, kernel, (1, 1, 1), 'VALID', dimension_numbers=('NCDHW', 'OIDHW', 'NCDHW'), preferred_element_type=jnp.float32)

def flipped(kernel):
    return jnp.transpose(kernel[:, :, ::-1, ::-1, ::-1], (1, 0, 2, 3, 4))

def filter_sums(source, target, upcast):
    result = conv_valid(source[:, None], target[:, None], upcast)
    return jnp.transpose(result, (1, 0, 2, 3, 4)).reshape(target.shape[0], -1)

def live_region(cell_flags, block_edge):
    position = jnp.arange(block_edge + 2)
    sub_part = (position >= 1).astype(jnp.int32) + (position >= block_edge + 1).astype(jnp.int32)
    selector = (sub_part[:, None] == jnp.arange(3)[None, :]).astype(jnp.float32)
    return jnp.einsum('ai,bj,ck,ijk->abc', selector, selector, selector, cell_flags)

def block_grads(padded_tile, cell_flags, conv1_weight, conv1_bias, conv2_weight, upcast):
    block_edge = padded_tile.shape[-1] - 4
    channels = conv1_weight.shape[0]
    first_kernel = conv1_weight.reshape(channels, channels, 3, 3, 3)
    second_kernel = conv2_weight.reshape(channels, channels, 3, 3, 3)
    features = padded_tile[0]
    upstream = padded_tile[1]
    live_mask = live_region(cell_flags, block_edge)
    pre_act = conv_valid(features[None], first_kernel, upcast)[0] + conv1_bias[:, None, None, None]
    sigmoid_pre = 1.0 / (1.0 + jnp.exp(-pre_act))
    hidden = (pre_act * sigmoid_pre * live_mask).astype(jnp.bfloat16)
    back_hidden = conv_valid(upstream[None], flipped(second_kernel), upcast)[0]
    grad_pre = (back_hidden * sigmoid_pre * (1.0 + pre_act * (1.0 - sigmoid_pre)) * live_mask).astype(jnp.bfloat16)
    inner_grad = grad_pre[:, 1:block_edge + 1, 1:block_edge + 1, 1:block_edge + 1]
    own_upstream = upstream[:, 2:block_edge + 2, 2:block_edge + 2, 2:block_edge + 2]
    spread_back = conv_valid(grad_pre[None], flipped(first_kernel), upcast)[0]
    grad_out = (own_upstream.astype(jnp.float32) + spread_back).astype(jnp.bfloat16).reshape(channels, -1)
    grad_first = filter_sums(features[:, 1:block_edge + 3, 1:block_edge + 3, 1:block_edge + 3], inner_grad, upcast)
    grad_second = filter_sums(hidden, own_upstream, upcast)
    grad_bias = lax.optimization_barrier(jnp.sum(inner_grad.astype(jnp.float32), axis=(1, 2, 3)))
    return (grad_out, grad_first, grad_second, grad_bias)

def reference(block_features, cotangent, coords, conv1_weight, conv1_bias, conv2_weight):
    fields = jnp.stack([block_features, cotangent], axis=1).reshape(SLOTS, 2, CH, BLOCK, BLOCK, BLOCK)
    step_table = jnp.asarray(neighbour_steps)
    slot_ids = jnp.arange(SLOTS, dtype=jnp.int32)
    valid_slot = coords[:, 0] >= 0

    def one_slot(slot_index):
        own_row = coords[slot_index]

        def compute_block(operand):
            targets = own_row[None, :] + step_table
            matched = jnp.all(coords[None, :, :] == targets[:, None, :], axis=2) & valid_slot[None, :]
            found = jnp.any(matched, axis=1)
            source_ids = lax.optimization_barrier(jnp.sum(jnp.where(matched, slot_ids[None, :], 0), axis=1)).astype(jnp.int32)
            neighbours = fields[source_ids]
            planes = []
            for x_step in range(3):
                row_list = []
                for y_step in range(3):
                    line_parts = []
                    for z_step in range(3):
                        offset_index = x_step * 9 + y_step * 3 + z_step
                        region = trimmed(neighbours[offset_index], x_step - 1, 2, BLOCK)
                        region = trimmed(region, y_step - 1, 3, BLOCK)
                        region = trimmed(region, z_step - 1, 4, BLOCK)
                        line_parts.append(jnp.where(found[offset_index], region, jnp.zeros_like(region)))
                    row_list.append(jnp.concatenate(line_parts, axis=4))
                planes.append(jnp.concatenate(row_list, axis=3))
            padded_tile = jnp.concatenate(planes, axis=2)
            cell_flags = found.astype(jnp.float32).reshape(3, 3, 3)
            return block_grads(padded_tile, cell_flags, conv1_weight, conv1_bias, conv2_weight, True)

        def empty_block(operand):
            return (jnp.zeros((CH, BLOCK ** 3), jnp.bfloat16), jnp.zeros((CH, 27 * CH), jnp.float32), jnp.zeros((CH, 27 * CH), jnp.float32), jnp.zeros((CH,), jnp.float32))
        return lax.cond(own_row[0] >= 0, compute_block, empty_block, 0)
    grad_rows, first_parts, second_parts, bias_parts = lax.map(one_slot, slot_ids)
    raw_first = lax.optimization_barrier(jnp.sum(first_parts, axis=0))
    raw_second = lax.optimization_barrier(jnp.sum(second_parts, axis=0))
    raw_bias = lax.optimization_barrier(jnp.sum(bias_parts, axis=0))
    norm_total = jnp.sqrt(jnp.sum(raw_first * raw_first) + jnp.sum(raw_second * raw_second) + jnp.sum(raw_bias * raw_bias))
    clip_scale = jnp.minimum(1.0, clip_norm / (norm_total + 1e-06))
    return (grad_rows, clip_scale * raw_first, clip_scale * raw_second, clip_scale * raw_bias)
```

```python
import jax
import jax.numpy as jnp
import numpy as np
from jax import lax
from jax.experimental import pallas as pl
from jax.experimental.pallas import tpu as pltpu
from jax.sharding import PartitionSpec as P

CH = 64
BLOCK = 16
EDGE = 20
PLANE = 512
LANES = 384
SHIFTS = tuple(dy * EDGE + dz for dy in range(3) for dz in range(3))

neighbour_steps = (
    np.stack(np.meshgrid(np.arange(-1, 2), np.arange(-1, 2), np.arange(-1, 2), indexing="ij"), -1)
    .reshape(27, 3)
    .astype(np.int32)
)
clip_norm = 256.0


def plane_tables():
    lane = np.arange(LANES)
    y, z = lane // EDGE, lane % EDGE
    ry = (y >= 1).astype(int) + (y >= 17).astype(int)
    rz = (z >= 1).astype(int) + (z >= 17).astype(int)
    inside = (y < 18) & (z < 18)
    regions = ((ry * 3 + rz)[None, :] == np.arange(9)[:, None]) & inside[None, :]
    inner = (y >= 1) & (y <= 16) & (z >= 1) & (z <= 16)
    own = (y < 16) & (z < 16)
    compress = (y * 16 + z)[:, None] == np.arange(256)[None, :]
    compress = compress & own[:, None]
    return (
        regions.astype(np.float32),
        np.stack([inner, own]).astype(np.float32),
        compress.astype(np.float32),
    )


def shifted(plane, lanes):
    parts = []
    for s in SHIFTS:
        if plane.shape[1] > lanes:
            parts.append(plane[:, s : s + lanes])
        elif s == 0:
            parts.append(plane)
        else:
            parts.append(jnp.concatenate([plane[:, s:], plane[:, :s]], axis=1))
    return jnp.concatenate(parts, axis=0)


def block_kernel(
    active_ref,
    tile_ref,
    live_ref,
    masks_ref,
    compress_ref,
    w1_ref,
    w2t_ref,
    w1t_ref,
    bias_ref,
    grad_ref,
    first_ref,
    second_ref,
    gbias_ref,
    px,
    pre,
    back,
    gin,
    gown,
    spread,
):
    slot = pl.program_id(0)

    @pl.when(slot == 0)
    def _():
        first_ref[...] = jnp.zeros_like(first_ref)
        second_ref[...] = jnp.zeros_like(second_ref)
        gbias_ref[...] = jnp.zeros_like(gbias_ref)

    live = active_ref[slot] > 0

    @pl.when(jnp.logical_not(live))
    def _():
        grad_ref[...] = jnp.zeros_like(grad_ref)

    @pl.when(live)
    def _():
        own_mask = masks_ref[1:2, :] > 0
        inner_mask = masks_ref[0:1, :] > 0
        zero = jnp.zeros((CH, LANES), jnp.bfloat16)
        for k in (0, 1, 18, 19):
            gown[k] = zero
        for k in (0, 1, 2, 19, 20):
            gin[k] = zero

        def conv_step(p, carry):
            xp = shifted(tile_ref[0, p, 0:CH, :], LANES)
            px[p] = xp
            r1 = jnp.dot(w1_ref[...], xp, preferred_element_type=jnp.float32)
            pre[p + 2] = r1[0:CH]
            pre[p + 1] = pre[p + 1] + r1[CH : 2 * CH]
            pre[p] = pre[p] + r1[2 * CH :]
            gp = shifted(tile_ref[0, p, CH : 2 * CH, :], LANES)
            r2 = jnp.dot(w2t_ref[...], gp, preferred_element_type=jnp.float32)
            back[p + 2] = r2[0:CH]
            back[p + 1] = back[p + 1] + r2[CH : 2 * CH]
            back[p] = back[p] + r2[2 * CH :]
            return carry

        lax.fori_loop(0, EDGE, conv_step, 0)

        def own_step(x, carry):
            plane = tile_ref[0, x + 2, CH : 2 * CH, :]
            own = plane[:, 42 : 42 + LANES]
            gown[x + 2] = jnp.where(own_mask, own, jnp.zeros_like(own))
            return carry

        lax.fori_loop(0, 16, own_step, 0)

        def mid_step(x, carry):
            region = (x >= 1).astype(jnp.int32) + (x >= 17).astype(jnp.int32)
            on = live_ref[0, region] > 0
            value = pre[x + 2] + bias_ref[...]
            sig = 1.0 / (1.0 + jnp.exp(-value))
            hidden = jnp.where(on, value * sig, 0.0).astype(jnp.bfloat16)
            gpre = back[x + 2] * sig * (1.0 + value * (1.0 - sig))
            gpre = jnp.where(on, gpre, 0.0).astype(jnp.bfloat16)
            inner = jnp.where(inner_mask, gpre, jnp.zeros_like(gpre))

            @pl.when(jnp.logical_and(x >= 1, x <= 16))
            def _():
                gin[x + 2] = inner
                gbias_ref[...] += jnp.sum(inner.astype(jnp.float32), axis=1, keepdims=True)

            r3 = jnp.dot(w1t_ref[...], shifted(gpre, LANES), preferred_element_type=jnp.float32)
            spread[x + 2] = r3[0:CH]
            spread[x + 1] = spread[x + 1] + r3[CH : 2 * CH]
            spread[x] = spread[x] + r3[2 * CH :]
            left = jnp.concatenate([gown[x + 2], gown[x + 1], gown[x]], axis=0)
            second_ref[...] += lax.dot_general(
                left,
                shifted(hidden, LANES),
                (((1,), (1,)), ((), ())),
                preferred_element_type=jnp.float32,
            )
            return carry

        lax.fori_loop(0, 18, mid_step, 0)

        def first_step(t, carry):
            left = jnp.concatenate([gin[t + 2], gin[t + 1], gin[t]], axis=0)
            first_ref[...] += lax.dot_general(
                left, px[t], (((1,), (1,)), ((), ())), preferred_element_type=jnp.float32
            )
            return carry

        lax.fori_loop(1, 19, first_step, 0)

        for x in range(16):
            plane = tile_ref[0, x + 2, CH : 2 * CH, :]
            own = plane[:, 42 : 42 + LANES].astype(jnp.float32)
            total = (own + spread[x + 2]).astype(jnp.bfloat16)
            grad_ref[0, :, x * 256 : (x + 1) * 256] = jnp.dot(
                total, compress_ref[...], preferred_element_type=jnp.float32
            ).astype(jnp.bfloat16)


def block_grads(active, tiles, live, w1, w2t, w1t, bias):
    _, masks, compress = plane_tables()
    whole2 = lambda s, a: (0, 0)
    wide = pl.BlockSpec((3 * CH, 9 * CH), whole2)
    return pl.pallas_call(
        block_kernel,
        grid_spec=pltpu.PrefetchScalarGridSpec(
            num_scalar_prefetch=1,
            grid=(2,),
            in_specs=[
                pl.BlockSpec((1, EDGE, 2 * CH, PLANE), lambda s, a: (s, 0, 0, 0)),
                pl.BlockSpec((1, 3, 1, LANES), lambda s, a: (s, 0, 0, 0)),
                pl.BlockSpec((2, LANES), whole2),
                pl.BlockSpec((LANES, 256), whole2),
                wide,
                wide,
                wide,
                pl.BlockSpec((CH, 1), whole2),
            ],
            out_specs=[
                pl.BlockSpec((1, CH, BLOCK**3), lambda s, a: (s, 0, 0)),
                wide,
                wide,
                pl.BlockSpec((CH, 1), whole2),
            ],
            scratch_shapes=[
                pltpu.VMEM((EDGE, 9 * CH, LANES), jnp.bfloat16),
                pltpu.VMEM((22, CH, LANES), jnp.float32),
                pltpu.VMEM((22, CH, LANES), jnp.float32),
                pltpu.VMEM((21, CH, LANES), jnp.bfloat16),
                pltpu.VMEM((20, CH, LANES), jnp.bfloat16),
                pltpu.VMEM((20, CH, LANES), jnp.float32),
            ],
        ),
        out_shape=[
            jax.ShapeDtypeStruct((2, CH, BLOCK**3), jnp.bfloat16),
            jax.ShapeDtypeStruct((3 * CH, 9 * CH), jnp.float32),
            jax.ShapeDtypeStruct((3 * CH, 9 * CH), jnp.float32),
            jax.ShapeDtypeStruct((CH, 1), jnp.float32),
        ],
        compiler_params=pltpu.CompilerParams(vmem_limit_bytes=56 * 2**20),
    )(
        active,
        tiles,
        live,
        jnp.asarray(masks),
        jnp.asarray(compress, jnp.bfloat16),
        w1,
        w2t,
        w1t,
        bias,
    )


def slot_matches(nearby, slot_index):
    own_row = nearby[2 + slot_index]
    targets = own_row[None, :] + jnp.asarray(neighbour_steps)
    grouped = jnp.repeat(nearby.reshape(3, 2, 3), 9, axis=0)
    return jnp.all(grouped == targets[:, None, :], axis=2) & (grouped[:, :, 0] >= 0)


def placement(nearby):
    cell = jnp.arange(256)
    lane = jnp.arange(PLANE)
    rows = nearby.reshape(3, 2, 3)
    own = rows[1]
    dy = rows[:, None, :, 1] - own[None, :, None, 1]
    dz = rows[:, None, :, 2] - own[None, :, None, 2]
    good = (rows[:, None, :, 0] >= 0) & (jnp.abs(dy) <= 1) & (jnp.abs(dz) <= 1)
    ty = (cell // 16) + 16 * dy[..., None] + 2
    tz = (cell % 16) + 16 * dz[..., None] + 2
    fits = good[..., None] & (ty >= 0) & (ty < EDGE) & (tz >= 0) & (tz < EDGE)
    target = jnp.where(fits, ty * EDGE + tz, -1)
    return (target[..., None] == lane).astype(jnp.bfloat16)


def conv_matrix(weight, transposed):
    kernel = weight.reshape(CH, CH, 3, 9)
    if transposed:
        kernel = jnp.transpose(kernel[:, :, ::-1, ::-1], (2, 1, 3, 0))
    else:
        kernel = jnp.transpose(kernel, (2, 0, 3, 1))
    return kernel.reshape(3 * CH, 9 * CH)


def weight_layout(raw):
    return jnp.transpose(raw.reshape(3, CH, 9, CH), (1, 3, 0, 2)).reshape(CH, 27 * CH)


def place(planes, maps):
    return jnp.einsum(
        "kcxa,skat->sxct", planes, maps, preferred_element_type=jnp.float32
    ).astype(jnp.bfloat16)


def body(block_features, cotangent, coords, conv1_weight, conv1_bias, conv2_weight):
    slab_index = lax.axis_index("space")
    count = lax.axis_size("space")
    forward = [(i, i + 1) for i in range(count - 1)]
    backward = [(target, source) for source, target in forward]
    fields = jnp.concatenate([block_features, cotangent], axis=1)
    low = lax.ppermute(fields[:, :, 14 * 256 :], "space", forward)
    high = lax.ppermute(fields[:, :, : 2 * 256], "space", backward)
    padded_coords = jnp.pad(coords, ((2, 2), (0, 0)), constant_values=-1)
    nearby = lax.dynamic_slice_in_dim(padded_coords, slab_index * 2, 6, 0)
    active = (nearby[2:4, 0] >= 0).astype(jnp.int32)
    maps = placement(nearby)
    tiles = jnp.concatenate(
        [
            place(low.reshape(2, 2 * CH, 2, 256), maps[0]),
            place(fields.reshape(2, 2 * CH, 16, 256), maps[1]),
            place(high.reshape(2, 2 * CH, 2, 256), maps[2]),
        ],
        axis=1,
    )
    regions, _, _ = plane_tables()
    flags = jnp.stack(
        [jnp.any(slot_matches(nearby, s), axis=1).astype(jnp.float32) for s in range(2)]
    )
    live = jnp.sum(flags.reshape(2, 3, 9, 1) * regions[None, None], axis=2)
    grad_features, first, second, gbias = block_grads(
        active,
        tiles,
        live.reshape(2, 3, 1, LANES),
        conv_matrix(conv1_weight, False),
        conv_matrix(conv2_weight, True),
        conv_matrix(conv1_weight, True),
        conv1_bias.reshape(CH, 1),
    )
    raw_first, raw_second, raw_bias = lax.psum((first, second, gbias), "space")
    norm_total = jnp.sqrt(
        jnp.sum(raw_first * raw_first)
        + jnp.sum(raw_second * raw_second)
        + jnp.sum(raw_bias * raw_bias)
    )
    clip_scale = jnp.minimum(1.0, clip_norm / (norm_total + 1e-06))
    return (
        grad_features,
        weight_layout(clip_scale * raw_first),
        weight_layout(clip_scale * raw_second),
        (clip_scale * raw_bias).reshape(CH),
    )


def solution(mesh):
    placed = (
        P(("groups", "space"), None, None),
        P(("groups", "space"), None, None),
        P("groups", None),
        P(),
        P(),
        P(),
    )
    return jax.shard_map(
        body,
        mesh=mesh,
        in_specs=placed,
        out_specs=(
            P(("groups", "space"), None, None),
            P("groups", None),
            P("groups", None),
            P("groups"),
        ),
        check_vma=False,
    )
```

```python
import jax
import jax.numpy as jnp
import numpy as np
from jax import lax
from jax.experimental import pallas as pl
from jax.experimental.pallas import tpu as pltpu
from jax.sharding import PartitionSpec as P

CH = 64
BLOCK = 16
EDGE = 20
PLANE = 512
LANES = 384
SHIFTS = tuple(dy * EDGE + dz for dy in range(3) for dz in range(3))

neighbour_steps = (
    np.stack(np.meshgrid(np.arange(-1, 2), np.arange(-1, 2), np.arange(-1, 2), indexing="ij"), -1)
    .reshape(27, 3)
    .astype(np.int32)
)
clip_norm = 256.0


def plane_tables():
    lane = np.arange(LANES)
    y, z = lane // EDGE, lane % EDGE
    ry = (y >= 1).astype(int) + (y >= 17).astype(int)
    rz = (z >= 1).astype(int) + (z >= 17).astype(int)
    inside = (y < 18) & (z < 18)
    regions = ((ry * 3 + rz)[None, :] == np.arange(9)[:, None]) & inside[None, :]
    inner = (y >= 1) & (y <= 16) & (z >= 1) & (z <= 16)
    own = (y < 16) & (z < 16)
    compress = (y * 16 + z)[:, None] == np.arange(256)[None, :]
    compress = compress & own[:, None]
    return (
        regions.astype(np.float32),
        np.stack([inner, own]).astype(np.float32),
        compress.astype(np.float32),
    )


def shifted(plane, lanes):
    parts = []
    for s in SHIFTS:
        if plane.shape[1] > lanes:
            parts.append(plane[:, s : s + lanes])
        elif s == 0:
            parts.append(plane)
        else:
            parts.append(jnp.concatenate([plane[:, s:], plane[:, :s]], axis=1))
    return jnp.concatenate(parts, axis=0)


def cell_sums(rows, columns):
    return lax.dot_general(
        rows, columns, (((1,), (1,)), ((), ())), preferred_element_type=jnp.float32
    )


def block_kernel(
    active_ref,
    tile_ref,
    live_ref,
    masks_ref,
    compress_ref,
    w1_ref,
    w2t_ref,
    w1t_ref,
    bias_ref,
    grad_ref,
    sums_ref,
    px,
    pre,
    back,
    gin,
    gown,
    spread,
    first,
    second,
    total_bias,
):
    slot = pl.program_id(0)

    @pl.when(slot == 0)
    def _():
        first[...] = jnp.zeros_like(first)
        second[...] = jnp.zeros_like(second)
        total_bias[...] = jnp.zeros_like(total_bias)

    live = active_ref[slot] > 0

    @pl.when(jnp.logical_not(live))
    def _():
        grad_ref[...] = jnp.zeros_like(grad_ref)

    @pl.when(live)
    def _():
        own_mask = masks_ref[1:2, :] > 0
        inner_mask = masks_ref[0:1, :] > 0
        zero = jnp.zeros((CH, LANES), jnp.bfloat16)
        for k in (0, 1, 18, 19):
            gown[k] = zero
        for k in (0, 1, 2, 19, 20):
            gin[k] = zero

        def conv_step(p, carry):
            xp = shifted(tile_ref[0, p, 0:CH, :], LANES)
            px[p] = xp
            r1 = jnp.dot(w1_ref[...], xp, preferred_element_type=jnp.float32)
            pre[p + 2] = r1[0:CH]
            pre[p + 1] = pre[p + 1] + r1[CH : 2 * CH]
            pre[p] = pre[p] + r1[2 * CH :]
            gp = shifted(tile_ref[0, p, CH : 2 * CH, :], LANES)
            r2 = jnp.dot(w2t_ref[...], gp, preferred_element_type=jnp.float32)
            back[p + 2] = r2[0:CH]
            back[p + 1] = back[p + 1] + r2[CH : 2 * CH]
            back[p] = back[p] + r2[2 * CH :]
            return carry

        lax.fori_loop(0, EDGE, conv_step, 0, unroll=2)

        def own_step(x, carry):
            plane = tile_ref[0, x + 2, CH : 2 * CH, :]
            own = plane[:, 42 : 42 + LANES]
            gown[x + 2] = jnp.where(own_mask, own, jnp.zeros_like(own))
            return carry

        lax.fori_loop(0, 16, own_step, 0, unroll=4)

        def mid_step(x, carry):
            region = (x >= 1).astype(jnp.int32) + (x >= 17).astype(jnp.int32)
            on = live_ref[0, region] > 0
            value = pre[x + 2] + bias_ref[...]
            sig = 1.0 / (1.0 + jnp.exp(-value))
            hidden = jnp.where(on, value * sig, 0.0).astype(jnp.bfloat16)
            gpre = back[x + 2] * sig * (1.0 + value * (1.0 - sig))
            gpre = jnp.where(on, gpre, 0.0).astype(jnp.bfloat16)
            inner = jnp.where(inner_mask, gpre, jnp.zeros_like(gpre))

            @pl.when(jnp.logical_and(x >= 1, x <= 16))
            def _():
                gin[x + 2] = inner

            r3 = jnp.dot(w1t_ref[...], shifted(gpre, LANES), preferred_element_type=jnp.float32)
            spread[x + 2] = r3[0:CH]
            spread[x + 1] = spread[x + 1] + r3[CH : 2 * CH]
            spread[x] = spread[x] + r3[2 * CH :]
            left = jnp.concatenate([gown[x + 2], gown[x + 1], gown[x]], axis=0)
            second[...] += cell_sums(shifted(hidden, LANES), left)
            return carry

        lax.fori_loop(0, 18, mid_step, 0, unroll=2)

        ones = jnp.ones((16, LANES), jnp.bfloat16)

        def first_step(t, carry):
            left = jnp.concatenate([gin[t + 2], gin[t + 1], gin[t]], axis=0)
            first[...] += cell_sums(px[t], left)
            total_bias[...] += cell_sums(ones, left)
            return carry

        lax.fori_loop(1, 19, first_step, 0, unroll=2)

        for x in range(16):
            plane = tile_ref[0, x + 2, CH : 2 * CH, :]
            own = plane[:, 42 : 42 + LANES].astype(jnp.float32)
            total = (own + spread[x + 2]).astype(jnp.bfloat16)
            grad_ref[0, :, x * 256 : (x + 1) * 256] = jnp.dot(
                total, compress_ref[...], preferred_element_type=jnp.float32
            ).astype(jnp.bfloat16)

    @pl.when(slot == 1)
    def _():
        sums_ref[0 : 9 * CH, :] = jnp.concatenate([first[...], second[...]], axis=1)
        row = total_bias[0:8, :]
        sums_ref[9 * CH :, :] = jnp.concatenate([row, row], axis=1)


def block_grads(active, tiles, live, w1, w2t, w1t, bias):
    _, masks, compress = plane_tables()
    whole2 = lambda s, a: (0, 0)
    wide = pl.BlockSpec((3 * CH, 9 * CH), whole2)
    return pl.pallas_call(
        block_kernel,
        grid_spec=pltpu.PrefetchScalarGridSpec(
            num_scalar_prefetch=1,
            grid=(2,),
            in_specs=[
                pl.BlockSpec((1, EDGE, 2 * CH, PLANE), lambda s, a: (s, 0, 0, 0)),
                pl.BlockSpec((1, 3, 1, LANES), lambda s, a: (s, 0, 0, 0)),
                pl.BlockSpec((2, LANES), whole2),
                pl.BlockSpec((LANES, 256), whole2),
                wide,
                wide,
                wide,
                pl.BlockSpec((CH, 1), whole2),
            ],
            out_specs=[
                pl.BlockSpec((1, CH, BLOCK**3), lambda s, a: (s, 0, 0)),
                pl.BlockSpec((9 * CH + 8, 6 * CH), whole2),
            ],
            scratch_shapes=[
                pltpu.VMEM((EDGE, 9 * CH, LANES), jnp.bfloat16),
                pltpu.VMEM((22, CH, LANES), jnp.float32),
                pltpu.VMEM((22, CH, LANES), jnp.float32),
                pltpu.VMEM((21, CH, LANES), jnp.bfloat16),
                pltpu.VMEM((20, CH, LANES), jnp.bfloat16),
                pltpu.VMEM((20, CH, LANES), jnp.float32),
                pltpu.VMEM((9 * CH, 3 * CH), jnp.float32),
                pltpu.VMEM((9 * CH, 3 * CH), jnp.float32),
                pltpu.VMEM((16, 3 * CH), jnp.float32),
            ],
        ),
        out_shape=[
            jax.ShapeDtypeStruct((2, CH, BLOCK**3), jnp.bfloat16),
            jax.ShapeDtypeStruct((9 * CH + 8, 6 * CH), jnp.float32),
        ],
        compiler_params=pltpu.CompilerParams(vmem_limit_bytes=56 * 2**20),
    )(
        active,
        tiles,
        live,
        jnp.asarray(masks),
        jnp.asarray(compress, jnp.bfloat16),
        w1,
        w2t,
        w1t,
        bias,
    )


def slot_matches(nearby, slot_index):
    own_row = nearby[2 + slot_index]
    targets = own_row[None, :] + jnp.asarray(neighbour_steps)
    grouped = jnp.repeat(nearby.reshape(3, 2, 3), 9, axis=0)
    return jnp.all(grouped == targets[:, None, :], axis=2) & (grouped[:, :, 0] >= 0)


def placement(nearby):
    cell = jnp.arange(256)
    lane = jnp.arange(PLANE)
    rows = nearby.reshape(3, 2, 3)
    own = rows[1]
    dy = rows[:, None, :, 1] - own[None, :, None, 1]
    dz = rows[:, None, :, 2] - own[None, :, None, 2]
    good = (rows[:, None, :, 0] >= 0) & (jnp.abs(dy) <= 1) & (jnp.abs(dz) <= 1)
    ty = (cell // 16) + 16 * dy[..., None] + 2
    tz = (cell % 16) + 16 * dz[..., None] + 2
    fits = good[..., None] & (ty >= 0) & (ty < EDGE) & (tz >= 0) & (tz < EDGE)
    target = jnp.where(fits, ty * EDGE + tz, -1)
    return (target[..., None] == lane).astype(jnp.bfloat16)


def conv_matrix(weight, transposed):
    kernel = weight.reshape(CH, CH, 3, 9)
    if transposed:
        kernel = jnp.transpose(kernel[:, :, ::-1, ::-1], (2, 1, 3, 0))
    else:
        kernel = jnp.transpose(kernel, (2, 0, 3, 1))
    return kernel.reshape(3 * CH, 9 * CH)


def weight_layout(raw):
    return jnp.transpose(raw.reshape(9, CH, 3, CH), (3, 1, 2, 0)).reshape(CH, 27 * CH)


def place(planes, maps):
    return jnp.einsum(
        "kcxa,skat->sxct", planes, maps, preferred_element_type=jnp.float32
    ).astype(jnp.bfloat16)


def body(block_features, cotangent, coords, conv1_weight, conv1_bias, conv2_weight):
    slab_index = lax.axis_index("space")
    count = lax.axis_size("space")
    forward = [(i, i + 1) for i in range(count - 1)]
    backward = [(target, source) for source, target in forward]
    fields = jnp.concatenate([block_features, cotangent], axis=1)
    low = lax.ppermute(fields[:, :, 14 * 256 :], "space", forward)
    high = lax.ppermute(fields[:, :, : 2 * 256], "space", backward)
    padded_coords = jnp.pad(coords, ((2, 2), (0, 0)), constant_values=-1)
    nearby = lax.dynamic_slice_in_dim(padded_coords, slab_index * 2, 6, 0)
    active = (nearby[2:4, 0] >= 0).astype(jnp.int32)
    maps = placement(nearby)
    tiles = jnp.concatenate(
        [
            place(low.reshape(2, 2 * CH, 2, 256), maps[0]),
            place(fields.reshape(2, 2 * CH, 16, 256), maps[1]),
            place(high.reshape(2, 2 * CH, 2, 256), maps[2]),
        ],
        axis=1,
    )
    regions, _, _ = plane_tables()
    flags = jnp.stack(
        [jnp.any(slot_matches(nearby, s), axis=1).astype(jnp.float32) for s in range(2)]
    )
    live = jnp.sum(flags.reshape(2, 3, 9, 1) * regions[None, None], axis=2)
    grad_features, sums = block_grads(
        active,
        tiles,
        live.reshape(2, 3, 1, LANES),
        conv_matrix(conv1_weight, False),
        conv_matrix(conv2_weight, True),
        conv_matrix(conv1_weight, True),
        conv1_bias.reshape(CH, 1),
    )
    sums = lax.psum(sums, "space")
    raw = sums[: 9 * CH]
    raw_bias = sums[9 * CH, :CH]
    norm_total = jnp.sqrt(jnp.sum(raw * raw) + jnp.sum(raw_bias * raw_bias))
    clip_scale = jnp.minimum(1.0, clip_norm / (norm_total + 1e-06))
    scaled = clip_scale * raw
    return (
        grad_features,
        weight_layout(scaled[:, : 3 * CH]),
        weight_layout(scaled[:, 3 * CH :]),
        clip_scale * raw_bias,
    )


def solution(mesh):
    placed = (
        P(("groups", "space"), None, None),
        P(("groups", "space"), None, None),
        P("groups", None),
        P(),
        P(),
        P(),
    )
    return jax.shard_map(
        body,
        mesh=mesh,
        in_specs=placed,
        out_specs=(
            P(("groups", "space"), None, None),
            P("groups", None),
            P("groups", None),
            P("groups"),
        ),
        check_vma=False,
    )
```

```python
import jax
import jax.numpy as jnp
import numpy as np
from jax import lax
from jax.experimental import pallas as pl
from jax.experimental.pallas import tpu as pltpu
from jax.sharding import PartitionSpec as P

CH = 64
BLOCK = 16
EDGE = 20
PLANE = 512
LANES = 384
SHIFTS = tuple(dy * EDGE + dz for dy in range(3) for dz in range(3))

neighbour_steps = (
    np.stack(np.meshgrid(np.arange(-1, 2), np.arange(-1, 2), np.arange(-1, 2), indexing="ij"), -1)
    .reshape(27, 3)
    .astype(np.int32)
)
clip_norm = 256.0


def plane_tables():
    lane = np.arange(LANES)
    y, z = lane // EDGE, lane % EDGE
    ry = (y >= 1).astype(int) + (y >= 17).astype(int)
    rz = (z >= 1).astype(int) + (z >= 17).astype(int)
    inside = (y < 18) & (z < 18)
    regions = ((ry * 3 + rz)[None, :] == np.arange(9)[:, None]) & inside[None, :]
    inner = (y >= 1) & (y <= 16) & (z >= 1) & (z <= 16)
    own = (y < 16) & (z < 16)
    compress = (y * 16 + z)[:, None] == np.arange(256)[None, :]
    compress = compress & own[:, None]
    return (
        regions.astype(np.float32),
        np.stack([inner, own]).astype(np.float32),
        compress.astype(np.float32),
    )


def shifted(plane, lanes):
    parts = []
    for s in SHIFTS:
        if plane.shape[1] > lanes:
            parts.append(plane[:, s : s + lanes])
        elif s == 0:
            parts.append(plane)
        else:
            parts.append(jnp.concatenate([plane[:, s:], plane[:, :s]], axis=1))
    return jnp.concatenate(parts, axis=0)


def cell_sums(rows, columns):
    return lax.dot_general(
        rows, columns, (((1,), (1,)), ((), ())), preferred_element_type=jnp.float32
    )


def block_kernel(
    active_ref,
    tile_ref,
    live_ref,
    masks_ref,
    compress_ref,
    w1_ref,
    w2t_ref,
    w1t_ref,
    bias_ref,
    grad_ref,
    sums_ref,
    px,
    pre,
    back,
    gin,
    gown,
    spread,
    first,
    second,
    total_bias,
):
    slot = pl.program_id(0)

    @pl.when(slot == 0)
    def _():
        first[...] = jnp.zeros_like(first)
        second[...] = jnp.zeros_like(second)
        total_bias[...] = jnp.zeros_like(total_bias)

    live = active_ref[slot] > 0

    @pl.when(jnp.logical_not(live))
    def _():
        grad_ref[...] = jnp.zeros_like(grad_ref)

    @pl.when(live)
    def _():
        own_mask = masks_ref[1:2, :] > 0
        inner_mask = masks_ref[0:1, :] > 0
        zero = jnp.zeros((CH, LANES), jnp.bfloat16)
        for k in (0, 1, 18, 19):
            gown[k] = zero
        for k in (0, 1, 2, 19, 20):
            gin[k] = zero

        def conv_step(p, carry):
            xp = shifted(tile_ref[0, p, 0:CH, :], LANES)
            px[p] = xp
            r1 = jnp.dot(w1_ref[...], xp, preferred_element_type=jnp.float32)
            pre[p + 2] = r1[0:CH]
            pre[p + 1] = pre[p + 1] + r1[CH : 2 * CH]
            pre[p] = pre[p] + r1[2 * CH :]
            gp = shifted(tile_ref[0, p, CH : 2 * CH, :], LANES)
            r2 = jnp.dot(w2t_ref[...], gp, preferred_element_type=jnp.float32)
            back[p + 2] = r2[0:CH]
            back[p + 1] = back[p + 1] + r2[CH : 2 * CH]
            back[p] = back[p] + r2[2 * CH :]
            return carry

        lax.fori_loop(0, EDGE, conv_step, 0, unroll=2)

        def own_step(x, carry):
            plane = tile_ref[0, x + 2, CH : 2 * CH, :]
            own = plane[:, 42 : 42 + LANES]
            gown[x + 2] = jnp.where(own_mask, own, jnp.zeros_like(own))
            return carry

        lax.fori_loop(0, 16, own_step, 0, unroll=4)

        def mid_step(x, carry):
            region = (x >= 1).astype(jnp.int32) + (x >= 17).astype(jnp.int32)
            on = live_ref[0, region] > 0
            value = pre[x + 2] + bias_ref[...]
            sig = 1.0 / (1.0 + jnp.exp(-value))
            hidden = jnp.where(on, value * sig, 0.0).astype(jnp.bfloat16)
            gpre = back[x + 2] * sig * (1.0 + value * (1.0 - sig))
            gpre = jnp.where(on, gpre, 0.0).astype(jnp.bfloat16)
            inner = jnp.where(inner_mask, gpre, jnp.zeros_like(gpre))

            @pl.when(jnp.logical_and(x >= 1, x <= 16))
            def _():
                gin[x + 2] = inner

            r3 = jnp.dot(w1t_ref[...], shifted(gpre, LANES), preferred_element_type=jnp.float32)
            spread[x + 2] = r3[0:CH]
            spread[x + 1] = spread[x + 1] + r3[CH : 2 * CH]
            spread[x] = spread[x] + r3[2 * CH :]
            left = jnp.concatenate([gown[x + 2], gown[x + 1], gown[x]], axis=0)
            second[...] += cell_sums(shifted(hidden, LANES), left)
            return carry

        lax.fori_loop(0, 18, mid_step, 0, unroll=2)

        ones = jnp.ones((16, LANES), jnp.bfloat16)

        def first_step(t, carry):
            left = jnp.concatenate([gin[t + 2], gin[t + 1], gin[t]], axis=0)
            first[...] += cell_sums(px[t], left)
            total_bias[...] += cell_sums(ones, left)
            return carry

        lax.fori_loop(1, 19, first_step, 0, unroll=2)

        for x in range(16):
            plane = tile_ref[0, x + 2, CH : 2 * CH, :]
            own = plane[:, 42 : 42 + LANES].astype(jnp.float32)
            total = (own + spread[x + 2]).astype(jnp.bfloat16)
            grad_ref[0, :, x * 256 : (x + 1) * 256] = jnp.dot(
                total, compress_ref[...], preferred_element_type=jnp.float32
            ).astype(jnp.bfloat16)

    @pl.when(slot == 1)
    def _():
        sums_ref[0 : 9 * CH, :] = jnp.concatenate([first[...], second[...]], axis=1)
        row = total_bias[0:8, :]
        sums_ref[9 * CH :, :] = jnp.concatenate([row, row], axis=1)


def block_grads(active, tiles, live, w1, w2t, w1t, bias):
    _, masks, compress = plane_tables()
    whole2 = lambda s, a: (0, 0)
    wide = pl.BlockSpec((3 * CH, 9 * CH), whole2)
    return pl.pallas_call(
        block_kernel,
        grid_spec=pltpu.PrefetchScalarGridSpec(
            num_scalar_prefetch=1,
            grid=(2,),
            in_specs=[
                pl.BlockSpec((1, EDGE, 2 * CH, PLANE), lambda s, a: (s, 0, 0, 0)),
                pl.BlockSpec((1, 3, 1, LANES), lambda s, a: (s, 0, 0, 0)),
                pl.BlockSpec((2, LANES), whole2),
                pl.BlockSpec((LANES, 256), whole2),
                wide,
                wide,
                wide,
                pl.BlockSpec((CH, 1), whole2),
            ],
            out_specs=[
                pl.BlockSpec((1, CH, BLOCK**3), lambda s, a: (s, 0, 0)),
                pl.BlockSpec((9 * CH + 8, 6 * CH), whole2),
            ],
            scratch_shapes=[
                pltpu.VMEM((EDGE, 9 * CH, LANES), jnp.bfloat16),
                pltpu.VMEM((22, CH, LANES), jnp.float32),
                pltpu.VMEM((22, CH, LANES), jnp.float32),
                pltpu.VMEM((21, CH, LANES), jnp.bfloat16),
                pltpu.VMEM((20, CH, LANES), jnp.bfloat16),
                pltpu.VMEM((20, CH, LANES), jnp.float32),
                pltpu.VMEM((9 * CH, 3 * CH), jnp.float32),
                pltpu.VMEM((9 * CH, 3 * CH), jnp.float32),
                pltpu.VMEM((16, 3 * CH), jnp.float32),
            ],
        ),
        out_shape=[
            jax.ShapeDtypeStruct((2, CH, BLOCK**3), jnp.bfloat16),
            jax.ShapeDtypeStruct((9 * CH + 8, 6 * CH), jnp.float32),
        ],
        compiler_params=pltpu.CompilerParams(vmem_limit_bytes=56 * 2**20),
    )(
        active,
        tiles,
        live,
        jnp.asarray(masks),
        jnp.asarray(compress, jnp.bfloat16),
        w1,
        w2t,
        w1t,
        bias,
    )


def slot_matches(nearby, slot_index):
    own_row = nearby[2 + slot_index]
    targets = own_row[None, :] + jnp.asarray(neighbour_steps)
    grouped = jnp.repeat(nearby.reshape(3, 2, 3), 9, axis=0)
    return jnp.all(grouped == targets[:, None, :], axis=2) & (grouped[:, :, 0] >= 0)


def placement(nearby):
    cell = jnp.arange(256)
    lane = jnp.arange(PLANE)
    rows = nearby.reshape(3, 2, 3)
    own = rows[1]
    dy = rows[:, None, :, 1] - own[None, :, None, 1]
    dz = rows[:, None, :, 2] - own[None, :, None, 2]
    good = (rows[:, None, :, 0] >= 0) & (jnp.abs(dy) <= 1) & (jnp.abs(dz) <= 1)
    ty = (cell // 16) + 16 * dy[..., None] + 2
    tz = (cell % 16) + 16 * dz[..., None] + 2
    fits = good[..., None] & (ty >= 0) & (ty < EDGE) & (tz >= 0) & (tz < EDGE)
    target = jnp.where(fits, ty * EDGE + tz, -1)
    return (target[..., None] == lane).astype(jnp.bfloat16)


def conv_matrix(weight, transposed):
    kernel = weight.reshape(CH, CH, 3, 9)
    if transposed:
        kernel = jnp.transpose(kernel[:, :, ::-1, ::-1], (2, 1, 3, 0))
    else:
        kernel = jnp.transpose(kernel, (2, 0, 3, 1))
    return kernel.reshape(3 * CH, 9 * CH)


def weight_layout(raw):
    return jnp.transpose(raw.reshape(9, CH, 3, CH), (3, 1, 2, 0)).reshape(CH, 27 * CH)


def place(planes, maps):
    return jnp.einsum(
        "kcxa,skat->sxct", planes, maps, preferred_element_type=jnp.float32
    ).astype(jnp.bfloat16)


def space_sum(values):
    count = lax.axis_size("space")
    if count & (count - 1):
        return lax.psum(values, "space")
    index = lax.axis_index("space")
    steps = count.bit_length() - 1
    rows = values.shape[0]
    whole = -(-rows // (8 * count)) * 8 * count
    held = jnp.pad(values, ((0, whole - rows), (0, 0)))
    for step in range(steps):
        pairs = [(i, i ^ (1 << step)) for i in range(count)]
        upper = ((index >> step) & 1) == 1
        half = held.shape[0] // 2
        low, high = held[:half], held[half:]
        sent = jnp.where(upper, low, high).astype(jnp.bfloat16)
        got = lax.ppermute(sent, "space", pairs)
        held = jnp.where(upper, high, low) + got.astype(jnp.float32)
    held = held.astype(jnp.bfloat16)
    for step in reversed(range(steps)):
        pairs = [(i, i ^ (1 << step)) for i in range(count)]
        upper = ((index >> step) & 1) == 1
        got = lax.ppermute(held, "space", pairs)
        held = jnp.concatenate([jnp.where(upper, got, held), jnp.where(upper, held, got)], axis=0)
    return held[:rows].astype(jnp.float32)


def body(block_features, cotangent, coords, conv1_weight, conv1_bias, conv2_weight):
    slab_index = lax.axis_index("space")
    count = lax.axis_size("space")
    forward = [(i, i + 1) for i in range(count - 1)]
    backward = [(target, source) for source, target in forward]
    fields = jnp.concatenate([block_features, cotangent], axis=1)
    low = lax.ppermute(fields[:, :, 14 * 256 :], "space", forward)
    high = lax.ppermute(fields[:, :, : 2 * 256], "space", backward)
    padded_coords = jnp.pad(coords, ((2, 2), (0, 0)), constant_values=-1)
    nearby = lax.dynamic_slice_in_dim(padded_coords, slab_index * 2, 6, 0)
    active = (nearby[2:4, 0] >= 0).astype(jnp.int32)
    maps = placement(nearby)
    tiles = jnp.concatenate(
        [
            place(low.reshape(2, 2 * CH, 2, 256), maps[0]),
            place(fields.reshape(2, 2 * CH, 16, 256), maps[1]),
            place(high.reshape(2, 2 * CH, 2, 256), maps[2]),
        ],
        axis=1,
    )
    regions, _, _ = plane_tables()
    flags = jnp.stack(
        [jnp.any(slot_matches(nearby, s), axis=1).astype(jnp.float32) for s in range(2)]
    )
    live = jnp.sum(flags.reshape(2, 3, 9, 1) * regions[None, None], axis=2)
    grad_features, sums = block_grads(
        active,
        tiles,
        live.reshape(2, 3, 1, LANES),
        conv_matrix(conv1_weight, False),
        conv_matrix(conv2_weight, True),
        conv_matrix(conv1_weight, True),
        conv1_bias.reshape(CH, 1),
    )
    sums = space_sum(sums)
    raw = sums[: 9 * CH]
    raw_bias = sums[9 * CH, :CH]
    norm_total = jnp.sqrt(jnp.sum(raw * raw) + jnp.sum(raw_bias * raw_bias))
    clip_scale = jnp.minimum(1.0, clip_norm / (norm_total + 1e-06))
    scaled = clip_scale * raw
    return (
        grad_features,
        weight_layout(scaled[:, : 3 * CH]),
        weight_layout(scaled[:, 3 * CH :]),
        clip_scale * raw_bias,
    )


def solution(mesh):
    placed = (
        P(("groups", "space"), None, None),
        P(("groups", "space"), None, None),
        P("groups", None),
        P(),
        P(),
        P(),
    )
    return jax.shard_map(
        body,
        mesh=mesh,
        in_specs=placed,
        out_specs=(
            P(("groups", "space"), None, None),
            P("groups", None),
            P("groups", None),
            P("groups"),
        ),
        check_vma=False,
    )
```

```python
import jax
import jax.numpy as jnp
import numpy as np
from jax import lax
from jax.experimental import pallas as pl
from jax.experimental.pallas import tpu as pltpu
from jax.sharding import PartitionSpec as P

CH = 64
BLOCK = 16
EDGE = 20
PLANE = 512
LANES = 384
SHIFTS = tuple(dy * EDGE + dz for dy in range(3) for dz in range(3))

neighbour_steps = (
    np.stack(np.meshgrid(np.arange(-1, 2), np.arange(-1, 2), np.arange(-1, 2), indexing="ij"), -1)
    .reshape(27, 3)
    .astype(np.int32)
)
clip_norm = 256.0


def plane_tables():
    lane = np.arange(LANES)
    y, z = lane // EDGE, lane % EDGE
    ry = (y >= 1).astype(int) + (y >= 17).astype(int)
    rz = (z >= 1).astype(int) + (z >= 17).astype(int)
    inside = (y < 18) & (z < 18)
    regions = ((ry * 3 + rz)[None, :] == np.arange(9)[:, None]) & inside[None, :]
    inner = (y >= 1) & (y <= 16) & (z >= 1) & (z <= 16)
    own = (y < 16) & (z < 16)
    compress = (y * 16 + z)[:, None] == np.arange(256)[None, :]
    compress = compress & own[:, None]
    return (
        regions.astype(np.float32),
        np.stack([inner, own]).astype(np.float32),
        compress.astype(np.float32),
    )


def shifted(plane, lanes):
    parts = []
    for s in SHIFTS:
        if plane.shape[1] > lanes:
            parts.append(plane[:, s : s + lanes])
        elif s == 0:
            parts.append(plane)
        else:
            parts.append(jnp.concatenate([plane[:, s:], plane[:, :s]], axis=1))
    return jnp.concatenate(parts, axis=0)


def cell_sums(rows, columns):
    return lax.dot_general(
        rows, columns, (((1,), (1,)), ((), ())), preferred_element_type=jnp.float32
    )


def block_kernel(
    active_ref,
    tile_ref,
    live_ref,
    masks_ref,
    compress_ref,
    w1_ref,
    w2t_ref,
    w1t_ref,
    bias_ref,
    grad_ref,
    sums_ref,
    px,
    pre,
    back,
    gin,
    gown,
    spread,
    first,
    second,
    total_bias,
):
    slot = pl.program_id(0)

    @pl.when(slot == 0)
    def _():
        first[...] = jnp.zeros_like(first)
        second[...] = jnp.zeros_like(second)
        total_bias[...] = jnp.zeros_like(total_bias)

    live = active_ref[slot] > 0

    @pl.when(jnp.logical_not(live))
    def _():
        grad_ref[...] = jnp.zeros_like(grad_ref)

    @pl.when(live)
    def _():
        own_mask = masks_ref[1:2, :] > 0
        inner_mask = masks_ref[0:1, :] > 0
        zero = jnp.zeros((CH, LANES), jnp.bfloat16)
        for k in (0, 1, 18, 19):
            gown[k] = zero
        for k in (0, 1, 2, 19, 20):
            gin[k] = zero

        def conv_step(p, carry):
            xp = shifted(tile_ref[0, p, 0:CH, :], LANES)
            px[p] = xp
            r1 = jnp.dot(w1_ref[...], xp, preferred_element_type=jnp.float32)
            pre[p + 2] = r1[0:CH]
            pre[p + 1] = pre[p + 1] + r1[CH : 2 * CH]
            pre[p] = pre[p] + r1[2 * CH :]
            gp = shifted(tile_ref[0, p, CH : 2 * CH, :], LANES)
            r2 = jnp.dot(w2t_ref[...], gp, preferred_element_type=jnp.float32)
            back[p + 2] = r2[0:CH]
            back[p + 1] = back[p + 1] + r2[CH : 2 * CH]
            back[p] = back[p] + r2[2 * CH :]
            return carry

        lax.fori_loop(0, EDGE, conv_step, 0, unroll=4)

        def own_step(x, carry):
            plane = tile_ref[0, x + 2, CH : 2 * CH, :]
            own = plane[:, 42 : 42 + LANES]
            gown[x + 2] = jnp.where(own_mask, own, jnp.zeros_like(own))
            return carry

        lax.fori_loop(0, 16, own_step, 0, unroll=4)

        def mid_step(x, carry):
            region = (x >= 1).astype(jnp.int32) + (x >= 17).astype(jnp.int32)
            on = live_ref[0, region] > 0
            value = pre[x + 2] + bias_ref[...]
            sig = 1.0 / (1.0 + jnp.exp(-value))
            hidden = jnp.where(on, value * sig, 0.0).astype(jnp.bfloat16)
            gpre = back[x + 2] * sig * (1.0 + value * (1.0 - sig))
            gpre = jnp.where(on, gpre, 0.0).astype(jnp.bfloat16)
            inner = jnp.where(inner_mask, gpre, jnp.zeros_like(gpre))

            @pl.when(jnp.logical_and(x >= 1, x <= 16))
            def _():
                gin[x + 2] = inner

            r3 = jnp.dot(w1t_ref[...], shifted(gpre, LANES), preferred_element_type=jnp.float32)
            spread[x + 2] = r3[0:CH]
            spread[x + 1] = spread[x + 1] + r3[CH : 2 * CH]
            spread[x] = spread[x] + r3[2 * CH :]
            left = jnp.concatenate([gown[x + 2], gown[x + 1], gown[x]], axis=0)
            second[...] += cell_sums(shifted(hidden, LANES), left)
            return carry

        lax.fori_loop(0, 18, mid_step, 0, unroll=3)

        ones = jnp.ones((16, LANES), jnp.bfloat16)

        def first_step(t, carry):
            left = jnp.concatenate([gin[t + 2], gin[t + 1], gin[t]], axis=0)
            first[...] += cell_sums(px[t], left)
            total_bias[...] += cell_sums(ones, left)
            return carry

        lax.fori_loop(1, 19, first_step, 0, unroll=3)

        for x in range(16):
            plane = tile_ref[0, x + 2, CH : 2 * CH, :]
            own = plane[:, 42 : 42 + LANES].astype(jnp.float32)
            total = (own + spread[x + 2]).astype(jnp.bfloat16)
            grad_ref[0, :, x * 256 : (x + 1) * 256] = jnp.dot(
                total, compress_ref[...], preferred_element_type=jnp.float32
            ).astype(jnp.bfloat16)

    @pl.when(slot == 1)
    def _():
        sums_ref[0 : 9 * CH, :] = jnp.concatenate([first[...], second[...]], axis=1)
        row = total_bias[0:8, :]
        sums_ref[9 * CH :, :] = jnp.concatenate([row, row], axis=1)


def block_grads(active, tiles, live, w1, w2t, w1t, bias):
    _, masks, compress = plane_tables()
    whole2 = lambda s, a: (0, 0)
    wide = pl.BlockSpec((3 * CH, 9 * CH), whole2)
    return pl.pallas_call(
        block_kernel,
        grid_spec=pltpu.PrefetchScalarGridSpec(
            num_scalar_prefetch=1,
            grid=(2,),
            in_specs=[
                pl.BlockSpec((1, EDGE, 2 * CH, PLANE), lambda s, a: (s, 0, 0, 0)),
                pl.BlockSpec((1, 3, 1, LANES), lambda s, a: (s, 0, 0, 0)),
                pl.BlockSpec((2, LANES), whole2),
                pl.BlockSpec((LANES, 256), whole2),
                wide,
                wide,
                wide,
                pl.BlockSpec((CH, 1), whole2),
            ],
            out_specs=[
                pl.BlockSpec((1, CH, BLOCK**3), lambda s, a: (s, 0, 0)),
                pl.BlockSpec((9 * CH + 8, 6 * CH), whole2),
            ],
            scratch_shapes=[
                pltpu.VMEM((EDGE, 9 * CH, LANES), jnp.bfloat16),
                pltpu.VMEM((22, CH, LANES), jnp.float32),
                pltpu.VMEM((22, CH, LANES), jnp.float32),
                pltpu.VMEM((21, CH, LANES), jnp.bfloat16),
                pltpu.VMEM((20, CH, LANES), jnp.bfloat16),
                pltpu.VMEM((20, CH, LANES), jnp.float32),
                pltpu.VMEM((9 * CH, 3 * CH), jnp.float32),
                pltpu.VMEM((9 * CH, 3 * CH), jnp.float32),
                pltpu.VMEM((16, 3 * CH), jnp.float32),
            ],
        ),
        out_shape=[
            jax.ShapeDtypeStruct((2, CH, BLOCK**3), jnp.bfloat16),
            jax.ShapeDtypeStruct((9 * CH + 8, 6 * CH), jnp.float32),
        ],
        compiler_params=pltpu.CompilerParams(vmem_limit_bytes=56 * 2**20),
    )(
        active,
        tiles,
        live,
        jnp.asarray(masks),
        jnp.asarray(compress, jnp.bfloat16),
        w1,
        w2t,
        w1t,
        bias,
    )


def slot_matches(nearby, slot_index):
    own_row = nearby[2 + slot_index]
    targets = own_row[None, :] + jnp.asarray(neighbour_steps)
    grouped = jnp.repeat(nearby.reshape(3, 2, 3), 9, axis=0)
    return jnp.all(grouped == targets[:, None, :], axis=2) & (grouped[:, :, 0] >= 0)


def placement(nearby):
    cell = jnp.arange(256)
    lane = jnp.arange(PLANE)
    rows = nearby.reshape(3, 2, 3)
    own = rows[1]
    dy = rows[:, None, :, 1] - own[None, :, None, 1]
    dz = rows[:, None, :, 2] - own[None, :, None, 2]
    good = (rows[:, None, :, 0] >= 0) & (jnp.abs(dy) <= 1) & (jnp.abs(dz) <= 1)
    ty = (cell // 16) + 16 * dy[..., None] + 2
    tz = (cell % 16) + 16 * dz[..., None] + 2
    fits = good[..., None] & (ty >= 0) & (ty < EDGE) & (tz >= 0) & (tz < EDGE)
    target = jnp.where(fits, ty * EDGE + tz, -1)
    return (target[..., None] == lane).astype(jnp.bfloat16)


def conv_matrix(weight, transposed):
    kernel = weight.reshape(CH, CH, 3, 9)
    if transposed:
        kernel = jnp.transpose(kernel[:, :, ::-1, ::-1], (2, 1, 3, 0))
    else:
        kernel = jnp.transpose(kernel, (2, 0, 3, 1))
    return kernel.reshape(3 * CH, 9 * CH)


def weight_layout(raw):
    return jnp.transpose(raw.reshape(9, CH, 3, CH), (3, 1, 2, 0)).reshape(CH, 27 * CH)


def place(planes, maps):
    return jnp.einsum(
        "kcxa,skat->sxct", planes, maps, preferred_element_type=jnp.float32
    ).astype(jnp.bfloat16)


def space_sum(values):
    count = lax.axis_size("space")
    if count & (count - 1):
        return lax.psum(values, "space")
    index = lax.axis_index("space")
    steps = count.bit_length() - 1
    rows = values.shape[0]
    whole = -(-rows // (8 * count)) * 8 * count
    held = jnp.pad(values, ((0, whole - rows), (0, 0)))
    for step in range(steps):
        pairs = [(i, i ^ (1 << step)) for i in range(count)]
        upper = ((index >> step) & 1) == 1
        half = held.shape[0] // 2
        low, high = held[:half], held[half:]
        sent = jnp.where(upper, low, high).astype(jnp.bfloat16)
        got = lax.ppermute(sent, "space", pairs)
        held = jnp.where(upper, high, low) + got.astype(jnp.float32)
    held = held.astype(jnp.bfloat16)
    for step in reversed(range(steps)):
        pairs = [(i, i ^ (1 << step)) for i in range(count)]
        upper = ((index >> step) & 1) == 1
        got = lax.ppermute(held, "space", pairs)
        held = jnp.concatenate([jnp.where(upper, got, held), jnp.where(upper, held, got)], axis=0)
    return held[:rows].astype(jnp.float32)


def body(block_features, cotangent, coords, conv1_weight, conv1_bias, conv2_weight):
    slab_index = lax.axis_index("space")
    count = lax.axis_size("space")
    forward = [(i, i + 1) for i in range(count - 1)]
    backward = [(target, source) for source, target in forward]
    fields = jnp.concatenate([block_features, cotangent], axis=1)
    low = lax.ppermute(fields[:, :, 14 * 256 :], "space", forward)
    high = lax.ppermute(fields[:, :, : 2 * 256], "space", backward)
    padded_coords = jnp.pad(coords, ((2, 2), (0, 0)), constant_values=-1)
    nearby = lax.dynamic_slice_in_dim(padded_coords, slab_index * 2, 6, 0)
    active = (nearby[2:4, 0] >= 0).astype(jnp.int32)
    maps = placement(nearby)
    tiles = jnp.concatenate(
        [
            place(low.reshape(2, 2 * CH, 2, 256), maps[0]),
            place(fields.reshape(2, 2 * CH, 16, 256), maps[1]),
            place(high.reshape(2, 2 * CH, 2, 256), maps[2]),
        ],
        axis=1,
    )
    regions, _, _ = plane_tables()
    flags = jnp.stack(
        [jnp.any(slot_matches(nearby, s), axis=1).astype(jnp.float32) for s in range(2)]
    )
    live = jnp.sum(flags.reshape(2, 3, 9, 1) * regions[None, None], axis=2)
    grad_features, sums = block_grads(
        active,
        tiles,
        live.reshape(2, 3, 1, LANES),
        conv_matrix(conv1_weight, False),
        conv_matrix(conv2_weight, True),
        conv_matrix(conv1_weight, True),
        conv1_bias.reshape(CH, 1),
    )
    sums = space_sum(sums)
    raw = sums[: 9 * CH]
    raw_bias = sums[9 * CH, :CH]
    norm_total = jnp.sqrt(jnp.sum(raw * raw) + jnp.sum(raw_bias * raw_bias))
    clip_scale = jnp.minimum(1.0, clip_norm / (norm_total + 1e-06))
    scaled = clip_scale * raw
    return (
        grad_features,
        weight_layout(scaled[:, : 3 * CH]),
        weight_layout(scaled[:, 3 * CH :]),
        clip_scale * raw_bias,
    )


def solution(mesh):
    placed = (
        P(("groups", "space"), None, None),
        P(("groups", "space"), None, None),
        P("groups", None),
        P(),
        P(),
        P(),
    )
    return jax.shard_map(
        body,
        mesh=mesh,
        in_specs=placed,
        out_specs=(
            P(("groups", "space"), None, None),
            P("groups", None),
            P("groups", None),
            P("groups"),
        ),
        check_vma=False,
    )
```
